32 devices in a mesh: grid: 16 (over z, y, core), orb: 2 (over x).
Axes of the slice: x: 2, y: 2, z: 4, core: 2. Of those that a mesh axis runs over, the one named last changes fastest.
Arguments:
- orbitals: bfloat16 [4096, 8192], P('grid', 'orb'), may hold values from -6 to 6
- points: int32 [1024], P('grid'), may hold values from 0 to 4095, as said below
Outputs:
- fitted: float32 [4096, 1024], P('grid', 'orb')
- gram: float32 [1024, 1024], P('grid', 'orb')
- density: float32 [1024], P('grid')
The draws below stay inside these ranges and needn't reach their ends.
Inputs may be any that keep to these rules, and one draw needn't show every extreme that they name: `points`: entries 64 * g to 64 * g + 63 are distinct grid rows of slab g, the rows 256 * g to 256 * g + 255.
All inputs are finite; a program needn't handle non-finite values.
Results may differ from the reference program's by a relative error of at most 0.0003.
Values may be sent and summed in bfloat16 or wider, within the bound.
A program may use at most 64 MiB of HBM per device.

```python
import jax
import jax.numpy as jnp
from jax import lax

NORB = 8192
ROWS_DEV = 256
MU_DEV = 64
NGRID = 4096
MU = 1024
N_GRID = 16


def draw_points(key, part):
    slabs = MU // MU_DEV
    keys = jax.random.split(jax.random.fold_in(key, 17), slabs)

    def one_slab(slab_key):
        return jax.random.permutation(slab_key, ROWS_DEV)[:MU_DEV].astype(jnp.int32)
    picks = jax.vmap(one_slab)(keys)
    slab_ids = jnp.arange(slabs, dtype=jnp.int32)
    firsts = picks[:, 0]
    shifts = jnp.where(slab_ids == 0, -firsts, jnp.zeros_like(firsts))
    shifts = jnp.where(slab_ids == slabs - 1, ROWS_DEV - 1 - firsts, shifts)
    picks = jnp.mod(picks + shifts[:, None], ROWS_DEV).astype(jnp.int32)
    offsets = (slab_ids * ROWS_DEV)[:, None]
    return (picks + offsets).reshape(MU).astype(jnp.int32)


def shard_levels(key, dims, pieces, smallest, high):
    loudness, own = 1.0, jax.random.fold_in(key, 6)
    for dim, parts in pieces:
        draws = jnp.exp(jax.random.uniform(jax.random.fold_in(own, dim), (parts,), jnp.float32, smallest / len(pieces), high / len(pieces)))
        loudness = loudness * jnp.repeat(draws, dims[dim] // parts).reshape([-1 if axis == dim else 1 for axis in range(len(dims))])
    return loudness


def scatter_about(rng, dims, deviation, bound, shards=(), kind=jnp.bfloat16):
    drawn = jax.random.normal(rng, dims, jnp.float32) * deviation
    if len(shards) > 0:
        drawn = shard_levels(rng, dims, shards, -0.22, 0.18) * drawn
    return jnp.clip(drawn, min=-bound, max=bound).astype(kind)


def setup_inputs(seed: int = 0) -> dict:
    key_list = jax.random.split(jax.random.key(seed), 3)
    orbitals = scatter_about(key_list[0], (NGRID, NORB), 1.0, 6.0, ((0, 16), (1, 2)))
    points = draw_points(jax.random.fold_in(key_list[2], 71), 0)
    return {"orbitals": orbitals, "points": points}


def reference(orbitals, points):
    chosen = jnp.take(orbitals, points, axis=0)
    chosen_wide = chosen.astype(jnp.float32)
    slabs = orbitals.reshape(N_GRID, ROWS_DEV, NORB)

    def slab_pair(block):
        return jnp.dot(block.astype(jnp.float32), chosen_wide.T, precision=lax.Precision.HIGHEST)
    pair = lax.map(slab_pair, slabs).reshape(N_GRID * ROWS_DEV, MU)
    correlation = jnp.dot(chosen_wide, chosen_wide.T, precision=lax.Precision.HIGHEST)
    scale = 1.0 / jnp.sqrt(jnp.float32(NORB))
    fitted = jnp.square(pair * scale)
    diagonal_mask = jnp.arange(MU)[:, None] == jnp.arange(MU)[None, :]
    gram = jnp.where(diagonal_mask, jnp.float32(0.0), jnp.square(correlation * scale))
    density = lax.optimization_barrier(jnp.sum(chosen_wide * chosen_wide, axis=1)) / jnp.float32(NORB)
    return (fitted, gram, density)
```

```python
import functools
import math

import jax
import jax.numpy as jnp
from jax import lax
from jax.experimental import pallas as pl
from jax.experimental.pallas import tpu as pltpu
from jax.sharding import PartitionSpec as P

MESH = pl.DeviceIdType.MESH
PIECE = 16


def contract(left, right):
    return lax.dot_general(
        left, right, (((1,), (1,)), ((), ())), preferred_element_type=jnp.float32
    )


def kernel(n_grid, n_orb, points_ref, a_ref, fitted_ref, gram_ref, density_ref,
           every, part, got, dens, up_sem, down_sem, side_sem, sib_sem, buddy_sem,
           recv_sem, part_send, part_recv, dens_send, dens_recv):
    rows, depth = a_ref.shape
    mu = every.shape[0] // n_grid
    layers = n_grid // 4
    pieces = mu // PIECE
    half = pieces // 2
    unit = 2 * mu
    local_units = (n_grid * mu) // n_orb // unit
    g = lax.axis_index("grid")
    o = lax.axis_index("orb")
    core, y, z = lax.rem(g, 2), lax.rem(g // 2, 2), g // 4
    buddy = z + 1 - 2 * lax.rem(z, 2)
    first, last = z == 0, z == layers - 1

    def device(zz, yy, cc):
        return zz * 4 + yy * 2 + cc

    barrier = pltpu.get_barrier_semaphore()

    def greet(where):
        pl.semaphore_signal(barrier, inc=1, device_id=where, device_id_type=MESH)

    @pl.when(jnp.logical_not(first))
    def _():
        greet({"grid": device(z - 1, y, core)})

    @pl.when(jnp.logical_not(last))
    def _():
        greet({"grid": device(z + 1, y, core)})

    greet({"grid": device(z, 1 - y, core)})
    greet({"grid": device(z, y, 1 - core)})
    for r in range(1, n_orb):
        greet({"orb": lax.rem(o + r, n_orb)})

    local = points_ref[...] - g * rows
    hot_t = (lax.broadcasted_iota(jnp.int32, (rows, mu), 0) == local).astype(jnp.float32)
    hot = jnp.transpose(hot_t)
    hot_narrow = hot.astype(jnp.bfloat16)
    chunk = min(depth, 1024)
    own_rows = pl.ds(pl.multiple_of(g * mu, mu), mu)

    def pick(k, total):
        cols = pl.ds(pl.multiple_of(k * chunk, chunk), chunk)
        wide = jnp.dot(hot_narrow, a_ref[:, cols], preferred_element_type=jnp.float32)
        every[own_rows, cols] = wide.astype(jnp.bfloat16)
        return total + jnp.sum(wide * wide, axis=1, keepdims=True)

    total = lax.fori_loop(0, depth // chunk, pick, jnp.zeros((mu, 1), jnp.float32))
    dens[o] = jnp.broadcast_to(total, (mu, 128))

    peers = n_orb + 1 + jnp.where(first, 0, 1) + jnp.where(last, 0, 1)
    pl.semaphore_wait(barrier, peers)

    def move(zz, yy, cc, p, target, sem):
        block = device(zz, yy, cc)
        piece = every.at[pl.ds(pl.multiple_of(block * mu + p * PIECE, PIECE), PIECE)]
        return pltpu.make_async_remote_copy(
            src_ref=piece, dst_ref=piece, send_sem=sem, recv_sem=recv_sem.at[block, p],
            device_id={"grid": target}, device_id_type=MESH,
        )

    def begin(copy):
        copy.start()

    def finish(copy):
        copy.wait_send()

    def to_up(zz, p, act):
        @pl.when(jnp.logical_not(last))
        def _():
            act(move(zz, y, core, p, device(z + 1, y, core), up_sem.at[zz, p]))

    def to_down(zz, p, act):
        @pl.when(jnp.logical_not(first))
        def _():
            act(move(zz, y, core, p, device(z - 1, y, core), down_sem.at[zz, p]))

    def to_side(zz, p, act):
        @pl.when(jnp.logical_or(zz != buddy, p >= half))
        def _():
            act(move(zz, y, core, p, device(z, 1 - y, core), side_sem.at[zz, p]))

    def to_sibling(zz, yy, p, act):
        act(move(zz, yy, core, p, device(z, y, 1 - core), sib_sem.at[zz * 2 + yy, p]))

    def to_buddy(p, act):
        act(move(z, 1 - y, core, p, device(buddy, y, core), buddy_sem.at[p]))

    def arrived(zz, yy, cc, p):
        move(zz, yy, cc, p, device(z, y, 1 - core), sib_sem.at[zz * 2 + yy, p]).wait_recv()

    def each(body, count=pieces, start=0):
        lax.fori_loop(start, count, lambda p, _: (body(p), 0)[1], 0)

    def on_layers(s, body):
        if s == 0:
            body(z)
        else:
            @pl.when(z - s >= 0)
            def _():
                body(z - s)

            @pl.when(z + s <= layers - 1)
            def _():
                body(z + s)

    def relay(s, act, wait):
        def below(p):
            if wait:
                arrived(z - s, y, core, p)
            to_up(z - s, p, act)
            to_side(z - s, p, act)
            to_sibling(z - s, y, p, act)

        def above(p):
            if wait:
                arrived(z + s, y, core, p)
            to_down(z + s, p, act)
            to_side(z + s, p, act)
            to_sibling(z + s, y, p, act)

        def both(p):
            @pl.when(z - s >= 0)
            def _():
                below(p)

            @pl.when(z + s <= layers - 1)
            def _():
                above(p)

        each(both)

    def from_side(s, act, wait):
        def one(p):
            def layer(zz):
                @pl.when(jnp.logical_or(zz != buddy, p >= half))
                def _():
                    if wait:
                        arrived(zz, 1 - y, core, p)
                    to_sibling(zz, 1 - y, p, act)

            on_layers(s, layer)

        each(one)

    def part_copy(u):
        owner = u // local_units
        lu = lax.rem(u, local_units)
        slot = lax.rem(o - owner + n_orb, n_orb) - 1
        return pltpu.make_async_remote_copy(
            src_ref=part.at[u], dst_ref=got.at[slot, lu], send_sem=part_send.at[u],
            recv_sem=part_recv.at[slot, lu], device_id={"orb": owner}, device_id_type=MESH,
        )

    def compute(zz, yy):
        each(lambda p: arrived(zz, yy, 1 - core, p))
        u = zz * 2 + yy
        span = pl.ds(pl.multiple_of(u * unit, unit), unit)

        def step(k, acc):
            cols = pl.ds(pl.multiple_of(k * chunk, chunk), chunk)
            return acc + contract(a_ref[:, cols], every[span, cols])

        part[u] = lax.fori_loop(0, depth // chunk, step, jnp.zeros((rows, unit), jnp.float32))

        @pl.when(u // local_units != o)
        def _():
            part_copy(u).start()

    def same_side(s):
        on_layers(s, lambda zz: compute(zz, y))

    def other_side(s, buddies):
        def layer(zz):
            @pl.when((zz == buddy) if buddies else (zz != buddy))
            def _():
                compute(zz, 1 - y)

        on_layers(s, layer)

    def own(act):
        def first_hops(p):
            to_up(z, p, act)
            to_down(z, p, act)
            to_side(z, p, act)

        each(first_hops)
        each(lambda p: to_sibling(z, y, p, act))

    own(begin)

    def dens_copy(r):
        return pltpu.make_async_remote_copy(
            src_ref=dens.at[o], dst_ref=dens.at[o], send_sem=dens_send.at[r - 1],
            recv_sem=dens_recv.at[o], device_id={"orb": lax.rem(o + r, n_orb)},
            device_id_type=MESH,
        )

    for r in range(1, n_orb):
        dens_copy(r).start()

    for s in range(1, layers):
        relay(s, begin, True)
        if s == max(layers - 2, 1):
            from_side(s - 1, begin, True)
            each(lambda p: to_buddy(p, begin), half)
        else:
            from_side(s - 1, begin, True)
        same_side(s - 1)
        if s >= 2:
            other_side(s - 2, False)

    same_side(layers - 1)
    other_side(layers - 2, False)
    from_side(layers - 1, begin, True)

    def buddy_in(act, wait):
        def one(p):
            if wait:
                arrived(buddy, 1 - y, core, p)
            to_sibling(buddy, 1 - y, p, act)

        each(one, half)

    buddy_in(begin, True)
    other_side(layers - 1, False)
    compute(buddy, 1 - y)

    scale = 1.0 / math.sqrt(depth * n_orb)
    for lu in range(local_units):
        u = o * local_units + lu
        pair = part[u]
        for slot in range(n_orb - 1):
            pltpu.make_async_remote_copy(
                src_ref=part.at[u], dst_ref=got.at[slot, lu], send_sem=part_send.at[u],
                recv_sem=part_recv.at[slot, lu], device_id={"orb": lax.rem(o + 1, n_orb)},
                device_id_type=MESH,
            ).wait_recv()
            pair = pair + got[slot, lu]
        cols = slice(lu * unit, (lu + 1) * unit)
        scaled = pair * scale
        fitted_ref[:, cols] = scaled * scaled
        over = jnp.dot(hot, scaled, preferred_element_type=jnp.float32,
                       precision=lax.Precision.HIGHEST)
        row_ids = g * mu + lax.broadcasted_iota(jnp.int32, (mu, unit), 0)
        col_ids = u * unit + lax.broadcasted_iota(jnp.int32, (mu, unit), 1)
        gram_ref[:, cols] = jnp.where(row_ids == col_ids, 0.0, over * over)

    for r in range(1, n_orb):
        peer = lax.rem(o + r, n_orb)
        pltpu.make_async_remote_copy(
            src_ref=dens.at[peer], dst_ref=dens.at[peer], send_sem=dens_send.at[r - 1],
            recv_sem=dens_recv.at[peer], device_id={"orb": peer}, device_id_type=MESH,
        ).wait_recv()
    whole = dens[0]
    for r in range(1, n_orb):
        whole = whole + dens[r]
    density_ref[...] = (jnp.transpose(whole) / jnp.float32(depth * n_orb))[0:1, :]

    own(finish)
    for s in range(1, layers):
        relay(s, finish, False)
        from_side(s - 1, finish, False)
    from_side(layers - 1, finish, False)
    each(lambda p: to_buddy(p, finish), half)
    buddy_in(finish, False)
    for r in range(1, n_orb):
        dens_copy(r).wait_send()

    def left(u, _):
        @pl.when(u // local_units != o)
        def _():
            part_copy(u).wait_send()

        return 0

    lax.fori_loop(0, 2 * layers, left, 0)


def solution(mesh):
    n_grid, n_orb = mesh.shape["grid"], mesh.shape["orb"]

    def on_device(orbitals, points):
        rows, depth = orbitals.shape
        mu = points.shape[0]
        layers = n_grid // 4
        pieces = mu // PIECE
        unit = 2 * mu
        width = n_grid * mu // n_orb
        dma = pltpu.SemaphoreType.DMA
        fitted, gram, density = pl.pallas_call(
            functools.partial(kernel, n_grid, n_orb),
            out_shape=(
                jax.ShapeDtypeStruct((rows, width), jnp.float32),
                jax.ShapeDtypeStruct((mu, width), jnp.float32),
                jax.ShapeDtypeStruct((1, mu), jnp.float32),
            ),
            in_specs=[pl.BlockSpec(memory_space=pltpu.VMEM)] * 2,
            out_specs=(pl.BlockSpec(memory_space=pltpu.VMEM),) * 3,
            scratch_shapes=[
                pltpu.VMEM((n_grid * mu, depth), jnp.bfloat16),
                pltpu.VMEM((2 * layers, rows, unit), jnp.float32),
                pltpu.VMEM((n_orb - 1, width // unit, rows, unit), jnp.float32),
                pltpu.VMEM((n_orb, mu, 128), jnp.float32),
                dma((layers, pieces)),
                dma((layers, pieces)),
                dma((layers, pieces)),
                dma((2 * layers, pieces)),
                dma((pieces,)),
                dma((n_grid, pieces)),
                dma((2 * layers,)),
                dma((n_orb - 1, width // unit)),
                dma((n_orb,)),
                dma((n_orb,)),
            ],
            compiler_params=pltpu.CompilerParams(
                collective_id=0, has_side_effects=True, vmem_limit_bytes=48 * 1024 * 1024
            ),
            cost_estimate=pl.CostEstimate(
                flops=2 * rows * depth * n_grid * mu,
                bytes_accessed=rows * depth * 2 + rows * width * 4,
                transcendentals=0,
            ),
        )(points.reshape(1, mu), orbitals)
        return fitted, gram, density.reshape(mu)

    return jax.shard_map(
        on_device,
        mesh=mesh,
        in_specs=(P("grid", "orb"), P("grid")),
        out_specs=(P("grid", "orb"), P("grid", "orb"), P("grid")),
        check_vma=False,
    )
```

```python
import functools
import math

import jax
import jax.numpy as jnp
from jax import lax
from jax.experimental import pallas as pl
from jax.experimental.pallas import tpu as pltpu
from jax.sharding import PartitionSpec as P

MESH = pl.DeviceIdType.MESH
PIECES = 4


def contract(left, right):
    return lax.dot_general(
        left, right, (((1,), (1,)), ((), ())), preferred_element_type=jnp.float32
    )


def kernel(n_grid, n_orb, points_hbm, a_hbm, pair_ref, hot_ref, density_ref,
           points_ref, a_ref, load_sem, every, part, got, dens, up_sem, down_sem, side_sem, sib_sem, buddy_sem,
           recv_sem, part_send, part_recv, dens_send, dens_recv):
    pieces, rows, chunk = a_ref.shape
    depth = pieces * chunk
    mu = every.shape[1] // n_grid
    layers = n_grid // 4
    half = pieces // 2
    unit = 2 * mu
    local_units = (n_grid * mu) // n_orb // unit
    g = lax.axis_index("grid")
    o = lax.axis_index("orb")
    core, y, z = lax.rem(g, 2), lax.rem(g // 2, 2), g // 4
    buddy = z + 1 - 2 * lax.rem(z, 2)
    first, last = z == 0, z == layers - 1

    def device(zz, yy, cc):
        return zz * 4 + yy * 2 + cc

    def load(p):
        return pltpu.make_async_copy(
            a_hbm.at[:, pl.ds(pl.multiple_of(p * chunk, 128), chunk)], a_ref.at[p],
            load_sem.at[p],
        )

    load_points = pltpu.make_async_copy(points_hbm, points_ref, load_sem.at[pieces])
    load_points.start()
    for p in range(pieces):
        load(p).start()

    barrier = pltpu.get_barrier_semaphore()

    def greet(where):
        pl.semaphore_signal(barrier, inc=1, device_id=where, device_id_type=MESH)

    @pl.when(jnp.logical_not(first))
    def _():
        greet({"grid": device(z - 1, y, core)})

    @pl.when(jnp.logical_not(last))
    def _():
        greet({"grid": device(z + 1, y, core)})

    greet({"grid": device(z, 1 - y, core)})
    greet({"grid": device(z, y, 1 - core)})
    for r in range(1, n_orb):
        greet({"orb": lax.rem(o + r, n_orb)})

    part[...] = jnp.zeros_like(part)
    load_points.wait()
    local = points_ref[...] - g * rows
    hot_t = (lax.broadcasted_iota(jnp.int32, (rows, mu), 0) == local).astype(jnp.float32)
    hot = jnp.transpose(hot_t)
    hot_ref[...] = hot
    hot_narrow = hot.astype(jnp.bfloat16)
    own_rows = pl.ds(pl.multiple_of(g * mu, mu), mu)

    peers = n_orb + 1 + jnp.where(first, 0, 1) + jnp.where(last, 0, 1)

    def move(zz, yy, cc, p, target, sem):
        block = device(zz, yy, cc)
        piece = every.at[p, pl.ds(pl.multiple_of(block * mu, mu), mu)]
        return pltpu.make_async_remote_copy(
            src_ref=piece, dst_ref=piece, send_sem=sem, recv_sem=recv_sem.at[block, p],
            device_id={"grid": target}, device_id_type=MESH,
        )

    def begin(copy):
        copy.start()

    def finish(copy):
        copy.wait_send()

    def to_up(zz, p, act):
        @pl.when(jnp.logical_not(last))
        def _():
            act(move(zz, y, core, p, device(z + 1, y, core), up_sem.at[zz, p]))

    def to_down(zz, p, act):
        @pl.when(jnp.logical_not(first))
        def _():
            act(move(zz, y, core, p, device(z - 1, y, core), down_sem.at[zz, p]))

    def to_side(zz, p, act):
        @pl.when(jnp.logical_or(zz != buddy, p >= half))
        def _():
            act(move(zz, y, core, p, device(z, 1 - y, core), side_sem.at[zz, p]))

    def to_sibling(zz, yy, p, act):
        act(move(zz, yy, core, p, device(z, y, 1 - core), sib_sem.at[zz * 2 + yy, p]))

    def to_buddy(p, act):
        act(move(z, 1 - y, core, p, device(buddy, y, core), buddy_sem.at[p]))

    def arrived(zz, yy, cc, p):
        move(zz, yy, cc, p, device(z, y, 1 - core), sib_sem.at[zz * 2 + yy, p]).wait_recv()

    def each(body, count=pieces, start=0):
        lax.fori_loop(start, count, lambda p, _: (body(p), 0)[1], 0)

    def on_layers(s, body):
        if s == 0:
            body(z)
        else:
            @pl.when(z - s >= 0)
            def _():
                body(z - s)

            @pl.when(z + s <= layers - 1)
            def _():
                body(z + s)

    def relay(s, act, wait):
        def below(p):
            if wait:
                arrived(z - s, y, core, p)
            to_up(z - s, p, act)
            to_side(z - s, p, act)
            to_sibling(z - s, y, p, act)

        def above(p):
            if wait:
                arrived(z + s, y, core, p)
            to_down(z + s, p, act)
            to_side(z + s, p, act)
            to_sibling(z + s, y, p, act)

        def both(p):
            @pl.when(z - s >= 0)
            def _():
                below(p)

            @pl.when(z + s <= layers - 1)
            def _():
                above(p)

        each(both)

    def by_side(zz, p):
        return jnp.logical_or(zz != buddy, p >= half)

    def from_side(s, act, wait):
        def one(p):
            def layer(zz):
                @pl.when(by_side(zz, p))
                def _():
                    if wait:
                        arrived(zz, 1 - y, core, p)
                    to_sibling(zz, 1 - y, p, act)

            on_layers(s, layer)

            if wait:
                @pl.when(p >= 1)
                def _():
                    on_layers(s, lambda zz: side_chunk(zz, p - 1))

        each(one)
        if wait:
            on_layers(s, lambda zz: side_chunk(zz, pieces - 1))

            def done(zz):
                @pl.when(zz != buddy)
                def _():
                    send_part(zz, 1 - y)

            on_layers(s, done)

    def part_copy(u):
        owner = u // local_units
        lu = lax.rem(u, local_units)
        slot = lax.rem(o - owner + n_orb, n_orb) - 1
        return pltpu.make_async_remote_copy(
            src_ref=part.at[u], dst_ref=got.at[slot, lu], send_sem=part_send.at[u],
            recv_sem=part_recv.at[slot, lu], device_id={"orb": owner}, device_id_type=MESH,
        )

    def multiply(zz, yy, p):
        arrived(zz, yy, 1 - core, p)
        u = zz * 2 + yy
        span = pl.ds(pl.multiple_of(u * unit, unit), unit)
        part[u] += contract(a_ref[p], every[p, span])

    def send_part(zz, yy):
        u = zz * 2 + yy

        @pl.when(u // local_units != o)
        def _():
            part_copy(u).start()

    def side_chunk(zz, p):
        @pl.when(by_side(zz, p))
        def _():
            multiply(zz, 1 - y, p)

    def same_side(s):
        def layer(zz):
            each(lambda p: multiply(zz, y, p))
            send_part(zz, y)

        on_layers(s, layer)

    def own(act):
        def first_hops(p):
            to_up(z, p, act)
            to_down(z, p, act)
            to_side(z, p, act)

        each(first_hops)
        each(lambda p: to_sibling(z, y, p, act))

    def pick(p):
        load(p).wait()
        wide = jnp.dot(hot_narrow, a_ref[p], preferred_element_type=jnp.float32)
        every[p, own_rows] = wide.astype(jnp.bfloat16)
        return jnp.sum(wide * wide, axis=1, keepdims=True)

    total = pick(0)
    pl.semaphore_wait(barrier, peers)
    for p in range(pieces):
        if p > 0:
            total = total + pick(p)
        to_up(z, p, begin)
        to_down(z, p, begin)
        to_side(z, p, begin)
        to_sibling(z, y, p, begin)
    dens[o] = jnp.broadcast_to(total, (mu, 128))

    def dens_copy(r):
        return pltpu.make_async_remote_copy(
            src_ref=dens.at[o], dst_ref=dens.at[o], send_sem=dens_send.at[r - 1],
            recv_sem=dens_recv.at[o], device_id={"orb": lax.rem(o + r, n_orb)},
            device_id_type=MESH,
        )

    for r in range(1, n_orb):
        dens_copy(r).start()

    for s in range(1, layers):
        relay(s, begin, True)
        if s == max(layers - 2, 1):
            if s == 1:
                from_side(0, begin, True)
            each(lambda p: to_buddy(p, begin), half)
            if s == 1:
                same_side(0)
                continue
        same_side(s - 1)
        from_side(s - 1, begin, True)

    same_side(layers - 1)

    def buddy_in(p, act, wait):
        if wait:
            arrived(buddy, 1 - y, core, p)
        to_sibling(buddy, 1 - y, p, act)

    def tail(p):
        def layer(zz):
            @pl.when(by_side(zz, p))
            def _():
                arrived(zz, 1 - y, core, p)
                to_sibling(zz, 1 - y, p, begin)

        on_layers(layers - 1, layer)

        @pl.when(p >= half)
        def _():
            buddy_in(p - half, begin, True)

        @pl.when(p >= 1)
        def _():
            on_layers(layers - 1, lambda zz: side_chunk(zz, p - 1))

        @pl.when(p >= half + 1)
        def _():
            multiply(buddy, 1 - y, p - half - 1)

    each(tail)
    on_layers(layers - 1, lambda zz: side_chunk(zz, pieces - 1))

    def done(zz):
        @pl.when(zz != buddy)
        def _():
            send_part(zz, 1 - y)

    on_layers(layers - 1, done)
    multiply(buddy, 1 - y, half - 1)
    send_part(buddy, 1 - y)

    scale = 1.0 / math.sqrt(depth * n_orb)
    for lu in range(local_units):
        u = o * local_units + lu
        pair = part[u]
        for slot in range(n_orb - 1):
            pltpu.make_async_remote_copy(
                src_ref=part.at[u], dst_ref=got.at[slot, lu], send_sem=part_send.at[u],
                recv_sem=part_recv.at[slot, lu], device_id={"orb": lax.rem(o + 1, n_orb)},
                device_id_type=MESH,
            ).wait_recv()
            pair = pair + got[slot, lu]
        cols = slice(lu * unit, (lu + 1) * unit)
        pair_ref[:, cols] = pair * scale

    for r in range(1, n_orb):
        peer = lax.rem(o + r, n_orb)
        pltpu.make_async_remote_copy(
            src_ref=dens.at[peer], dst_ref=dens.at[peer], send_sem=dens_send.at[r - 1],
            recv_sem=dens_recv.at[peer], device_id={"orb": peer}, device_id_type=MESH,
        ).wait_recv()
    whole = dens[0]
    for r in range(1, n_orb):
        whole = whole + dens[r]
    density_ref[...] = whole / jnp.float32(depth * n_orb)

    own(finish)
    for s in range(1, layers):
        relay(s, finish, False)
        from_side(s - 1, finish, False)
    from_side(layers - 1, finish, False)
    each(lambda p: to_buddy(p, finish), half)
    each(lambda p: buddy_in(p, finish, False), half)
    for r in range(1, n_orb):
        dens_copy(r).wait_send()

    def left(u, _):
        @pl.when(u // local_units != o)
        def _():
            part_copy(u).wait_send()

        return 0

    lax.fori_loop(0, 2 * layers, left, 0)


def outputs(pair_hbm, hot_hbm, dens_hbm, fitted_ref, gram_ref, density_ref,
            pair_ref, hot_ref, dens_ref, sems):
    loads = [
        pltpu.make_async_copy(src, dst, sems.at[i])
        for i, (src, dst) in enumerate(
            [(pair_hbm, pair_ref), (hot_hbm, hot_ref), (dens_hbm, dens_ref)]
        )
    ]
    for load in loads:
        load.start()
    for load in loads:
        load.wait()
    mu, width = gram_ref.shape
    pair = pair_ref[...]
    fitted_ref[...] = pair * pair
    over = jnp.dot(hot_ref[...], pair, preferred_element_type=jnp.float32,
                   precision=lax.Precision.HIGHEST)
    row_ids = lax.axis_index("grid") * mu + lax.broadcasted_iota(jnp.int32, (mu, width), 0)
    col_ids = lax.axis_index("orb") * width + lax.broadcasted_iota(jnp.int32, (mu, width), 1)
    gram_ref[...] = jnp.where(row_ids == col_ids, 0.0, over * over)
    density_ref[...] = jnp.transpose(dens_ref[...])[0:1, :]


def solution(mesh):
    n_grid, n_orb = mesh.shape["grid"], mesh.shape["orb"]

    def on_device(orbitals, points):
        rows, depth = orbitals.shape
        mu = points.shape[0]
        layers = n_grid // 4
        pieces = PIECES
        chunk = depth // pieces
        unit = 2 * mu
        width = n_grid * mu // n_orb
        dma = pltpu.SemaphoreType.DMA
        vmem = pl.BlockSpec(memory_space=pltpu.VMEM)
        pair, hot, dens = pl.pallas_call(
            functools.partial(kernel, n_grid, n_orb),
            out_shape=(
                jax.ShapeDtypeStruct((rows, width), jnp.float32),
                jax.ShapeDtypeStruct((mu, rows), jnp.float32),
                jax.ShapeDtypeStruct((mu, 128), jnp.float32),
            ),
            in_specs=[pl.BlockSpec(memory_space=pltpu.HBM)] * 2,
            out_specs=(vmem,) * 3,
            scratch_shapes=[
                pltpu.VMEM((1, mu), jnp.int32),
                pltpu.VMEM((pieces, rows, chunk), jnp.bfloat16),
                dma((pieces + 1,)),
                pltpu.VMEM((pieces, n_grid * mu, chunk), jnp.bfloat16),
                pltpu.VMEM((2 * layers, rows, unit), jnp.float32),
                pltpu.VMEM((n_orb - 1, width // unit, rows, unit), jnp.float32),
                pltpu.VMEM((n_orb, mu, 128), jnp.float32),
                dma((layers, pieces)),
                dma((layers, pieces)),
                dma((layers, pieces)),
                dma((2 * layers, pieces)),
                dma((pieces,)),
                dma((n_grid, pieces)),
                dma((2 * layers,)),
                dma((n_orb - 1, width // unit)),
                dma((n_orb,)),
                dma((n_orb,)),
            ],
            compiler_params=pltpu.CompilerParams(
                collective_id=0, has_side_effects=True, vmem_limit_bytes=60 * 1024 * 1024
            ),
            cost_estimate=pl.CostEstimate(
                flops=2 * rows * depth * n_grid * mu,
                bytes_accessed=rows * depth * 2 + rows * width * 4,
                transcendentals=0,
            ),
        )(points.reshape(1, mu), orbitals)
        fitted, gram, density = pl.pallas_call(
            outputs,
            out_shape=(
                jax.ShapeDtypeStruct((rows, width), jnp.float32),
                jax.ShapeDtypeStruct((mu, width), jnp.float32),
                jax.ShapeDtypeStruct((1, mu), jnp.float32),
            ),
            in_specs=[pl.BlockSpec(memory_space=pl.ANY)] * 3,
            out_specs=(vmem,) * 3,
            scratch_shapes=[
                pltpu.VMEM((rows, width), jnp.float32),
                pltpu.VMEM((mu, rows), jnp.float32),
                pltpu.VMEM((mu, 128), jnp.float32),
                dma((3,)),
            ],
            compiler_params=pltpu.CompilerParams(vmem_limit_bytes=60 * 1024 * 1024),
        )(pair, hot, dens)
        return fitted, gram, density.reshape(mu)

    return jax.shard_map(
        on_device,
        mesh=mesh,
        in_specs=(P("grid", "orb"), P("grid")),
        out_specs=(P("grid", "orb"), P("grid", "orb"), P("grid")),
        check_vma=False,
    )
```

```python
import functools
import math

import jax
import jax.numpy as jnp
from jax import lax
from jax.experimental import pallas as pl
from jax.experimental.pallas import tpu as pltpu
from jax.sharding import PartitionSpec as P

MESH = pl.DeviceIdType.MESH
PIECES = 4


def contract(left, right):
    return lax.dot_general(
        left, right, (((1,), (1,)), ((), ())), preferred_element_type=jnp.float32
    )


def kernel(n_grid, n_orb, points_hbm, a_hbm, fitted_ref, gram_ref, density_ref,
           points_ref, a_ref, load_sem, every, part, got, dens, up_sem, down_sem, side_sem, sib_sem, buddy_sem,
           recv_sem, part_send, part_recv, dens_send, dens_recv):
    pieces, rows, chunk = a_ref.shape
    depth = pieces * chunk
    mu = every.shape[1] // n_grid
    layers = n_grid // 4
    half = pieces // 2
    unit = 2 * mu
    local_units = (n_grid * mu) // n_orb // unit
    g = lax.axis_index("grid")
    o = lax.axis_index("orb")
    core, y, z = lax.rem(g, 2), lax.rem(g // 2, 2), g // 4
    buddy = z + 1 - 2 * lax.rem(z, 2)
    first, last = z == 0, z == layers - 1

    def device(zz, yy, cc):
        return zz * 4 + yy * 2 + cc

    def load(p):
        return pltpu.make_async_copy(
            a_hbm.at[:, pl.ds(pl.multiple_of(p * chunk, 128), chunk)], a_ref.at[p],
            load_sem.at[p],
        )

    load_points = pltpu.make_async_copy(points_hbm, points_ref, load_sem.at[pieces])
    load_points.start()
    for p in range(pieces):
        load(p).start()

    barrier = pltpu.get_barrier_semaphore()

    def greet(where):
        pl.semaphore_signal(barrier, inc=1, device_id=where, device_id_type=MESH)

    @pl.when(jnp.logical_not(first))
    def _():
        greet({"grid": device(z - 1, y, core)})

    @pl.when(jnp.logical_not(last))
    def _():
        greet({"grid": device(z + 1, y, core)})

    greet({"grid": device(z, 1 - y, core)})
    greet({"grid": device(z, y, 1 - core)})
    for r in range(1, n_orb):
        greet({"orb": lax.rem(o + r, n_orb)})

    part[...] = jnp.zeros_like(part)
    load_points.wait()
    local = points_ref[...] - g * rows
    hot_t = (lax.broadcasted_iota(jnp.int32, (rows, mu), 0) == local).astype(jnp.float32)
    hot = jnp.transpose(hot_t)
    hot_narrow = hot.astype(jnp.bfloat16)
    own_rows = pl.ds(pl.multiple_of(g * mu, mu), mu)

    peers = n_orb + 1 + jnp.where(first, 0, 1) + jnp.where(last, 0, 1)

    def move(zz, yy, cc, p, target, sem):
        block = device(zz, yy, cc)
        piece = every.at[p, pl.ds(pl.multiple_of(block * mu, mu), mu)]
        return pltpu.make_async_remote_copy(
            src_ref=piece, dst_ref=piece, send_sem=sem, recv_sem=recv_sem.at[block, p],
            device_id={"grid": target}, device_id_type=MESH,
        )

    def begin(copy):
        copy.start()

    def finish(copy):
        copy.wait_send()

    def to_up(zz, p, act):
        @pl.when(jnp.logical_not(last))
        def _():
            act(move(zz, y, core, p, device(z + 1, y, core), up_sem.at[zz, p]))

    def to_down(zz, p, act):
        @pl.when(jnp.logical_not(first))
        def _():
            act(move(zz, y, core, p, device(z - 1, y, core), down_sem.at[zz, p]))

    def to_side(zz, p, act):
        @pl.when(jnp.logical_or(zz != buddy, p >= half))
        def _():
            act(move(zz, y, core, p, device(z, 1 - y, core), side_sem.at[zz, p]))

    def to_sibling(zz, yy, p, act):
        act(move(zz, yy, core, p, device(z, y, 1 - core), sib_sem.at[zz * 2 + yy, p]))

    def to_buddy(p, act):
        act(move(z, 1 - y, core, p, device(buddy, y, core), buddy_sem.at[p]))

    def arrived(zz, yy, cc, p):
        move(zz, yy, cc, p, device(z, y, 1 - core), sib_sem.at[zz * 2 + yy, p]).wait_recv()

    def each(body, count=pieces, start=0):
        lax.fori_loop(start, count, lambda p, _: (body(p), 0)[1], 0)

    def on_layers(s, body):
        if s == 0:
            body(z)
        else:
            @pl.when(z - s >= 0)
            def _():
                body(z - s)

            @pl.when(z + s <= layers - 1)
            def _():
                body(z + s)

    def relay(s, act, wait):
        def below(p):
            if wait:
                arrived(z - s, y, core, p)
            to_up(z - s, p, act)
            to_side(z - s, p, act)
            to_sibling(z - s, y, p, act)

        def above(p):
            if wait:
                arrived(z + s, y, core, p)
            to_down(z + s, p, act)
            to_side(z + s, p, act)
            to_sibling(z + s, y, p, act)

        def both(p):
            @pl.when(z - s >= 0)
            def _():
                below(p)

            @pl.when(z + s <= layers - 1)
            def _():
                above(p)

        each(both)

    def by_side(zz, p):
        return jnp.logical_or(zz != buddy, p >= half)

    def from_side(s, act, wait):
        def one(p):
            def layer(zz):
                @pl.when(by_side(zz, p))
                def _():
                    if wait:
                        arrived(zz, 1 - y, core, p)
                    to_sibling(zz, 1 - y, p, act)

            on_layers(s, layer)

            if wait:
                @pl.when(p >= 1)
                def _():
                    on_layers(s, lambda zz: side_chunk(zz, p - 1))

        each(one)
        if wait:
            on_layers(s, lambda zz: side_chunk(zz, pieces - 1))

            def done(zz):
                @pl.when(zz != buddy)
                def _():
                    send_part(zz, 1 - y)

            on_layers(s, done)

    def part_copy(u):
        owner = u // local_units
        lu = lax.rem(u, local_units)
        slot = lax.rem(o - owner + n_orb, n_orb) - 1
        return pltpu.make_async_remote_copy(
            src_ref=part.at[u], dst_ref=got.at[slot, lu], send_sem=part_send.at[u],
            recv_sem=part_recv.at[slot, lu], device_id={"orb": owner}, device_id_type=MESH,
        )

    def multiply(zz, yy, p):
        arrived(zz, yy, 1 - core, p)
        u = zz * 2 + yy
        span = pl.ds(pl.multiple_of(u * unit, unit), unit)
        part[u] += contract(a_ref[p], every[p, span])

    def send_part(zz, yy):
        u = zz * 2 + yy

        @pl.when(u // local_units != o)
        def _():
            part_copy(u).start()

    def side_chunk(zz, p):
        @pl.when(by_side(zz, p))
        def _():
            multiply(zz, 1 - y, p)

    def same_side(s):
        def layer(zz):
            each(lambda p: multiply(zz, y, p))
            send_part(zz, y)

        on_layers(s, layer)

    def own(act):
        def first_hops(p):
            to_up(z, p, act)
            to_down(z, p, act)
            to_side(z, p, act)

        each(first_hops)
        each(lambda p: to_sibling(z, y, p, act))

    def pick(p):
        load(p).wait()
        wide = jnp.dot(hot_narrow, a_ref[p], preferred_element_type=jnp.float32)
        every[p, own_rows] = wide.astype(jnp.bfloat16)
        return jnp.sum(wide * wide, axis=1, keepdims=True)

    total = pick(0)
    pl.semaphore_wait(barrier, peers)
    for p in range(pieces):
        if p > 0:
            total = total + pick(p)
        to_up(z, p, begin)
        to_down(z, p, begin)
        to_side(z, p, begin)
        to_sibling(z, y, p, begin)
    dens[o] = jnp.broadcast_to(total, (mu, 128))

    def dens_copy(r):
        return pltpu.make_async_remote_copy(
            src_ref=dens.at[o], dst_ref=dens.at[o], send_sem=dens_send.at[r - 1],
            recv_sem=dens_recv.at[o], device_id={"orb": lax.rem(o + r, n_orb)},
            device_id_type=MESH,
        )

    for r in range(1, n_orb):
        dens_copy(r).start()

    for s in range(1, layers):
        relay(s, begin, True)
        if s == max(layers - 2, 1):
            if s == 1:
                from_side(0, begin, True)
            each(lambda p: to_buddy(p, begin), half)
            if s == 1:
                same_side(0)
                continue
        same_side(s - 1)
        from_side(s - 1, begin, True)

    same_side(layers - 1)

    def buddy_in(p, act, wait):
        if wait:
            arrived(buddy, 1 - y, core, p)
        to_sibling(buddy, 1 - y, p, act)

    def tail(p):
        def layer(zz):
            @pl.when(by_side(zz, p))
            def _():
                arrived(zz, 1 - y, core, p)
                to_sibling(zz, 1 - y, p, begin)

        on_layers(layers - 1, layer)

        @pl.when(p >= half)
        def _():
            buddy_in(p - half, begin, True)

        @pl.when(p >= 1)
        def _():
            on_layers(layers - 1, lambda zz: side_chunk(zz, p - 1))

        @pl.when(p >= half + 1)
        def _():
            multiply(buddy, 1 - y, p - half - 1)

    each(tail)
    on_layers(layers - 1, lambda zz: side_chunk(zz, pieces - 1))

    def done(zz):
        @pl.when(zz != buddy)
        def _():
            send_part(zz, 1 - y)

    on_layers(layers - 1, done)
    multiply(buddy, 1 - y, half - 1)
    send_part(buddy, 1 - y)

    own(finish)
    for s in range(1, layers):
        relay(s, finish, False)
        from_side(s - 1, finish, False)
    from_side(layers - 1, finish, False)
    each(lambda p: to_buddy(p, finish), half)
    each(lambda p: buddy_in(p, finish, False), half)
    for r in range(1, n_orb):
        dens_copy(r).wait_send()

    for r in range(1, n_orb):
        peer = lax.rem(o + r, n_orb)
        pltpu.make_async_remote_copy(
            src_ref=dens.at[peer], dst_ref=dens.at[peer], send_sem=dens_send.at[r - 1],
            recv_sem=dens_recv.at[peer], device_id={"orb": peer}, device_id_type=MESH,
        ).wait_recv()
    whole = dens[0]
    for r in range(1, n_orb):
        whole = whole + dens[r]
    density_ref[...] = (jnp.transpose(whole) / jnp.float32(depth * n_orb))[0:1, :]

    scale = 1.0 / math.sqrt(depth * n_orb)
    local_layers = local_units // 2
    row_ids = g * mu + lax.broadcasted_iota(jnp.int32, (mu, unit), 0)
    lane_ids = lax.broadcasted_iota(jnp.int32, (mu, unit), 1)
    for j in range(local_units):
        i = j % local_layers
        layer = jnp.where(z < layers // 2, i, local_layers - 1 - i)
        lu = layer * 2 + (y if j < local_layers else 1 - y)
        u = o * local_units + lu
        pair = part[u]
        for slot in range(n_orb - 1):
            pltpu.make_async_remote_copy(
                src_ref=part.at[u], dst_ref=got.at[slot, lu], send_sem=part_send.at[u],
                recv_sem=part_recv.at[slot, lu], device_id={"orb": lax.rem(o + 1, n_orb)},
                device_id_type=MESH,
            ).wait_recv()
            pair = pair + got[slot, lu]
        cols = pl.ds(pl.multiple_of(lu * unit, unit), unit)
        scaled = pair * scale
        fitted_ref[:, cols] = scaled * scaled
        over = jnp.dot(hot, scaled, preferred_element_type=jnp.float32,
                       precision=lax.Precision.HIGHEST)
        gram_ref[:, cols] = jnp.where(row_ids == u * unit + lane_ids, 0.0, over * over)

    def left(u, _):
        @pl.when(u // local_units != o)
        def _():
            part_copy(u).wait_send()

        return 0

    lax.fori_loop(0, 2 * layers, left, 0)


def copies(a_from, b_from, c_from, a_to, b_to, c_to, sems):
    moves = [
        pltpu.make_async_copy(a_from, a_to, sems.at[0]),
        pltpu.make_async_copy(b_from, b_to, sems.at[1]),
        pltpu.make_async_copy(c_from, c_to, sems.at[2]),
    ]
    for move in moves:
        move.start()
    for move in moves:
        move.wait()


def solution(mesh):
    n_grid, n_orb = mesh.shape["grid"], mesh.shape["orb"]

    def on_device(orbitals, points):
        rows, depth = orbitals.shape
        mu = points.shape[0]
        layers = n_grid // 4
        pieces = PIECES
        chunk = depth // pieces
        unit = 2 * mu
        width = n_grid * mu // n_orb
        dma = pltpu.SemaphoreType.DMA
        vmem = pl.BlockSpec(memory_space=pltpu.VMEM)
        made = pl.pallas_call(
            functools.partial(kernel, n_grid, n_orb),
            out_shape=(
                jax.ShapeDtypeStruct((rows, width), jnp.float32),
                jax.ShapeDtypeStruct((mu, width), jnp.float32),
                jax.ShapeDtypeStruct((1, mu), jnp.float32),
            ),
            in_specs=[pl.BlockSpec(memory_space=pltpu.HBM)] * 2,
            out_specs=(vmem,) * 3,
            scratch_shapes=[
                pltpu.VMEM((1, mu), jnp.int32),
                pltpu.VMEM((pieces, rows, chunk), jnp.bfloat16),
                dma((pieces + 1,)),
                pltpu.VMEM((pieces, n_grid * mu, chunk), jnp.bfloat16),
                pltpu.VMEM((2 * layers, rows, unit), jnp.float32),
                pltpu.VMEM((n_orb - 1, width // unit, rows, unit), jnp.float32),
                pltpu.VMEM((n_orb, mu, 128), jnp.float32),
                dma((layers, pieces)),
                dma((layers, pieces)),
                dma((layers, pieces)),
                dma((2 * layers, pieces)),
                dma((pieces,)),
                dma((n_grid, pieces)),
                dma((2 * layers,)),
                dma((n_orb - 1, width // unit)),
                dma((n_orb,)),
                dma((n_orb,)),
            ],
            compiler_params=pltpu.CompilerParams(
                collective_id=0, has_side_effects=True, vmem_limit_bytes=60 * 1024 * 1024
            ),
            cost_estimate=pl.CostEstimate(
                flops=2 * rows * depth * n_grid * mu,
                bytes_accessed=rows * depth * 2 + rows * width * 4,
                transcendentals=0,
            ),
        )(points.reshape(1, mu), orbitals)
        fitted, gram, density = pl.pallas_call(
            copies,
            out_shape=tuple(jax.ShapeDtypeStruct(m.shape, m.dtype) for m in made),
            in_specs=[pl.BlockSpec(memory_space=pl.ANY)] * 3,
            out_specs=(pl.BlockSpec(memory_space=pl.ANY),) * 3,
            scratch_shapes=[dma((3,))],
            compiler_params=pltpu.CompilerParams(vmem_limit_bytes=60 * 1024 * 1024),
        )(*made)
        return fitted, gram, density.reshape(mu)

    return jax.shard_map(
        on_device,
        mesh=mesh,
        in_specs=(P("grid", "orb"), P("grid")),
        out_specs=(P("grid", "orb"), P("grid", "orb"), P("grid")),
        check_vma=False,
    )
```

```python
import functools
import math

import jax
import jax.numpy as jnp
from jax import lax
from jax.experimental import pallas as pl
from jax.experimental.pallas import tpu as pltpu
from jax.sharding import PartitionSpec as P

MESH = pl.DeviceIdType.MESH
PIECES = 4


def contract(left, right):
    return lax.dot_general(
        left, right, (((1,), (1,)), ((), ())), preferred_element_type=jnp.float32
    )


def kernel(n_grid, n_orb, points_hbm, a_hbm, fitted_ref, gram_ref, density_ref,
           points_ref, a_ref, load_sem, every, part, got, dens, up_sem, down_sem, side_sem, sib_sem, buddy_sem,
           recv_sem, part_send, part_recv, dens_send, dens_recv):
    pieces, rows, chunk = a_ref.shape
    depth = pieces * chunk
    mu = every.shape[1] // n_grid
    layers = n_grid // 4
    half = pieces // 2
    unit = 2 * mu
    local_units = (n_grid * mu) // n_orb // unit
    g = lax.axis_index("grid")
    o = lax.axis_index("orb")
    core, y, z = lax.rem(g, 2), lax.rem(g // 2, 2), g // 4
    buddy = z + 1 - 2 * lax.rem(z, 2)
    first, last = z == 0, z == layers - 1

    def device(zz, yy, cc):
        return zz * 4 + yy * 2 + cc

    def load(p):
        return pltpu.make_async_copy(
            a_hbm.at[:, pl.ds(pl.multiple_of(p * chunk, 128), chunk)], a_ref.at[p],
            load_sem.at[p],
        )

    load_points = pltpu.make_async_copy(points_hbm, points_ref, load_sem.at[pieces])
    load_points.start()
    for p in range(pieces):
        load(p).start()

    barrier = pltpu.get_barrier_semaphore()

    def greet(where):
        pl.semaphore_signal(barrier, inc=1, device_id=where, device_id_type=MESH)

    @pl.when(jnp.logical_not(first))
    def _():
        greet({"grid": device(z - 1, y, core)})

    @pl.when(jnp.logical_not(last))
    def _():
        greet({"grid": device(z + 1, y, core)})

    greet({"grid": device(z, 1 - y, core)})
    greet({"grid": device(z, y, 1 - core)})
    for r in range(1, n_orb):
        greet({"orb": lax.rem(o + r, n_orb)})

    part[...] = jnp.zeros_like(part)
    load_points.wait()
    local = points_ref[...] - g * rows
    hot_t = (lax.broadcasted_iota(jnp.int32, (rows, mu), 0) == local).astype(jnp.float32)
    hot = jnp.transpose(hot_t)
    hot_narrow = hot.astype(jnp.bfloat16)
    own_rows = pl.ds(pl.multiple_of(g * mu, mu), mu)

    peers = n_orb + 1 + jnp.where(first, 0, 1) + jnp.where(last, 0, 1)

    def move(zz, yy, cc, p, target, sem):
        block = device(zz, yy, cc)
        piece = every.at[p, pl.ds(pl.multiple_of(block * mu, mu), mu)]
        return pltpu.make_async_remote_copy(
            src_ref=piece, dst_ref=piece, send_sem=sem, recv_sem=recv_sem.at[block, p],
            device_id={"grid": target}, device_id_type=MESH,
        )

    def begin(copy):
        copy.start()

    def finish(copy):
        copy.wait_send()

    def to_up(zz, p, act):
        @pl.when(jnp.logical_not(last))
        def _():
            act(move(zz, y, core, p, device(z + 1, y, core), up_sem.at[zz, p]))

    def to_down(zz, p, act):
        @pl.when(jnp.logical_not(first))
        def _():
            act(move(zz, y, core, p, device(z - 1, y, core), down_sem.at[zz, p]))

    def to_side(zz, p, act):
        @pl.when(jnp.logical_or(zz != buddy, p >= half))
        def _():
            act(move(zz, y, core, p, device(z, 1 - y, core), side_sem.at[zz, p]))

    def to_sibling(zz, yy, p, act):
        act(move(zz, yy, core, p, device(z, y, 1 - core), sib_sem.at[zz * 2 + yy, p]))

    def to_buddy(p, act):
        act(move(z, 1 - y, core, p, device(buddy, y, core), buddy_sem.at[p]))

    def arrived(zz, yy, cc, p):
        move(zz, yy, cc, p, device(z, y, 1 - core), sib_sem.at[zz * 2 + yy, p]).wait_recv()

    def each(body, count=pieces, start=0):
        lax.fori_loop(start, count, lambda p, _: (body(p), 0)[1], 0)

    def on_layers(s, body):
        if s == 0:
            body(z)
        else:
            @pl.when(z - s >= 0)
            def _():
                body(z - s)

            @pl.when(z + s <= layers - 1)
            def _():
                body(z + s)

    def relay(s, act, wait):
        def below(p):
            if wait:
                arrived(z - s, y, core, p)
            to_up(z - s, p, act)
            to_side(z - s, p, act)
            to_sibling(z - s, y, p, act)

        def above(p):
            if wait:
                arrived(z + s, y, core, p)
            to_down(z + s, p, act)
            to_side(z + s, p, act)
            to_sibling(z + s, y, p, act)

        def both(p):
            @pl.when(z - s >= 0)
            def _():
                below(p)

            @pl.when(z + s <= layers - 1)
            def _():
                above(p)

        each(both)

    def by_side(zz, p):
        return jnp.logical_or(zz != buddy, p >= half)

    def from_side(s, act, wait):
        def one(p):
            def layer(zz):
                @pl.when(by_side(zz, p))
                def _():
                    if wait:
                        arrived(zz, 1 - y, core, p)
                    to_sibling(zz, 1 - y, p, act)

            on_layers(s, layer)

            if wait:
                @pl.when(p >= 1)
                def _():
                    on_layers(s, lambda zz: side_chunk(zz, p - 1))

        each(one)
        if wait:
            on_layers(s, lambda zz: side_chunk(zz, pieces - 1))

            def done(zz):
                @pl.when(zz != buddy)
                def _():
                    send_part(zz, 1 - y)

            on_layers(s, done)

    def part_copy(u):
        owner = u // local_units
        lu = lax.rem(u, local_units)
        slot = lax.rem(o - owner + n_orb, n_orb) - 1
        return pltpu.make_async_remote_copy(
            src_ref=part.at[u], dst_ref=got.at[slot, lu], send_sem=part_send.at[u],
            recv_sem=part_recv.at[slot, lu], device_id={"orb": owner}, device_id_type=MESH,
        )

    def multiply(zz, yy, p):
        arrived(zz, yy, 1 - core, p)
        u = zz * 2 + yy
        span = pl.ds(pl.multiple_of(u * unit, unit), unit)
        part[u] += contract(a_ref[p], every[p, span])

    def send_part(zz, yy):
        u = zz * 2 + yy

        @pl.when(u // local_units != o)
        def _():
            part_copy(u).start()

    def side_chunk(zz, p):
        @pl.when(by_side(zz, p))
        def _():
            multiply(zz, 1 - y, p)

    def same_side(s):
        def layer(zz):
            each(lambda p: multiply(zz, y, p))
            send_part(zz, y)

        on_layers(s, layer)

    def own(act):
        def first_hops(p):
            to_up(z, p, act)
            to_down(z, p, act)
            to_side(z, p, act)

        each(first_hops)
        each(lambda p: to_sibling(z, y, p, act))

    def pick(p):
        load(p).wait()
        wide = jnp.dot(hot_narrow, a_ref[p], preferred_element_type=jnp.float32)
        every[p, own_rows] = wide.astype(jnp.bfloat16)
        return jnp.sum(wide * wide, axis=1, keepdims=True)

    total = pick(0)
    pl.semaphore_wait(barrier, peers)
    for p in range(pieces):
        if p > 0:
            total = total + pick(p)
        to_up(z, p, begin)
        to_down(z, p, begin)
        to_side(z, p, begin)
        to_sibling(z, y, p, begin)
    dens[o] = jnp.broadcast_to(total, (mu, 128))

    def dens_copy(r):
        return pltpu.make_async_remote_copy(
            src_ref=dens.at[o], dst_ref=dens.at[o], send_sem=dens_send.at[r - 1],
            recv_sem=dens_recv.at[o], device_id={"orb": lax.rem(o + r, n_orb)},
            device_id_type=MESH,
        )

    for r in range(1, n_orb):
        dens_copy(r).start()

    for s in range(1, layers):
        relay(s, begin, True)
        if s == max(layers - 2, 1):
            if s == 1:
                from_side(0, begin, True)
            each(lambda p: to_buddy(p, begin), half)
            if s == 1:
                same_side(0)
                continue
        same_side(s - 1)
        from_side(s - 1, begin, True)

    same_side(layers - 1)

    def buddy_in(p, act, wait):
        if wait:
            arrived(buddy, 1 - y, core, p)
        to_sibling(buddy, 1 - y, p, act)

    def tail(p):
        def layer(zz):
            @pl.when(by_side(zz, p))
            def _():
                arrived(zz, 1 - y, core, p)
                to_sibling(zz, 1 - y, p, begin)

        on_layers(layers - 1, layer)

        @pl.when(p >= half)
        def _():
            buddy_in(p - half, begin, True)

        @pl.when(p >= 1)
        def _():
            on_layers(layers - 1, lambda zz: side_chunk(zz, p - 1))

        @pl.when(p >= half + 1)
        def _():
            multiply(buddy, 1 - y, p - half - 1)

    each(tail)
    on_layers(layers - 1, lambda zz: side_chunk(zz, pieces - 1))

    def done(zz):
        @pl.when(zz != buddy)
        def _():
            send_part(zz, 1 - y)

    on_layers(layers - 1, done)
    multiply(buddy, 1 - y, half - 1)
    send_part(buddy, 1 - y)

    own(finish)
    for s in range(1, layers):
        relay(s, finish, False)
        from_side(s - 1, finish, False)
    from_side(layers - 1, finish, False)
    each(lambda p: to_buddy(p, finish), half)
    each(lambda p: buddy_in(p, finish, False), half)
    for r in range(1, n_orb):
        dens_copy(r).wait_send()

    for r in range(1, n_orb):
        peer = lax.rem(o + r, n_orb)
        pltpu.make_async_remote_copy(
            src_ref=dens.at[peer], dst_ref=dens.at[peer], send_sem=dens_send.at[r - 1],
            recv_sem=dens_recv.at[peer], device_id={"orb": peer}, device_id_type=MESH,
        ).wait_recv()
    whole = dens[0]
    for r in range(1, n_orb):
        whole = whole + dens[r]
    density_ref[...] = (jnp.transpose(whole) / jnp.float32(depth * n_orb))[0:1, :]

    scale = 1.0 / math.sqrt(depth * n_orb)
    local_layers = local_units // 2
    row_ids = g * mu + lax.broadcasted_iota(jnp.int32, (mu, unit), 0)
    lane_ids = lax.broadcasted_iota(jnp.int32, (mu, unit), 1)
    for j in range(local_units):
        i = j % local_layers
        layer = jnp.where(z < layers // 2, i, local_layers - 1 - i)
        lu = layer * 2 + (y if j < local_layers else 1 - y)
        u = o * local_units + lu
        pair = part[u]
        for slot in range(n_orb - 1):
            pltpu.make_async_remote_copy(
                src_ref=part.at[u], dst_ref=got.at[slot, lu], send_sem=part_send.at[u],
                recv_sem=part_recv.at[slot, lu], device_id={"orb": lax.rem(o + 1, n_orb)},
                device_id_type=MESH,
            ).wait_recv()
            pair = pair + got[slot, lu]
        cols = pl.ds(pl.multiple_of(lu * unit, unit), unit)
        scaled = pair * scale
        fitted_ref[:, cols] = scaled * scaled
        over = jnp.dot(hot, scaled, preferred_element_type=jnp.float32,
                       precision=lax.Precision.HIGHEST)
        gram_ref[:, cols] = jnp.where(row_ids == u * unit + lane_ids, 0.0, over * over)

    def left(u, _):
        @pl.when(u // local_units != o)
        def _():
            part_copy(u).wait_send()

        return 0

    lax.fori_loop(0, 2 * layers, left, 0)


def copies(*refs):
    sources, targets, held, sems = refs[:3], refs[3:6], refs[6:9], refs[9]
    loads = [pltpu.make_async_copy(sources[i], held[i], sems.at[i]) for i in range(3)]
    stores = [pltpu.make_async_copy(held[i], targets[i], sems.at[3 + i]) for i in range(3)]
    for load in loads:
        load.start()
    for load, store in zip(loads, stores):
        load.wait()
        store.start()
    for store in stores:
        store.wait()


def solution(mesh):
    n_grid, n_orb = mesh.shape["grid"], mesh.shape["orb"]

    def on_device(orbitals, points):
        rows, depth = orbitals.shape
        mu = points.shape[0]
        layers = n_grid // 4
        pieces = PIECES
        chunk = depth // pieces
        unit = 2 * mu
        width = n_grid * mu // n_orb
        dma = pltpu.SemaphoreType.DMA
        vmem = pl.BlockSpec(memory_space=pltpu.VMEM)
        made = pl.pallas_call(
            functools.partial(kernel, n_grid, n_orb),
            out_shape=(
                jax.ShapeDtypeStruct((rows, width), jnp.float32),
                jax.ShapeDtypeStruct((mu, width), jnp.float32),
                jax.ShapeDtypeStruct((1, mu), jnp.float32),
            ),
            in_specs=[pl.BlockSpec(memory_space=pltpu.HBM)] * 2,
            out_specs=(vmem,) * 3,
            scratch_shapes=[
                pltpu.VMEM((1, mu), jnp.int32),
                pltpu.VMEM((pieces, rows, chunk), jnp.bfloat16),
                dma((pieces + 1,)),
                pltpu.VMEM((pieces, n_grid * mu, chunk), jnp.bfloat16),
                pltpu.VMEM((2 * layers, rows, unit), jnp.float32),
                pltpu.VMEM((n_orb - 1, width // unit, rows, unit), jnp.float32),
                pltpu.VMEM((n_orb, mu, 128), jnp.float32),
                dma((layers, pieces)),
                dma((layers, pieces)),
                dma((layers, pieces)),
                dma((2 * layers, pieces)),
                dma((pieces,)),
                dma((n_grid, pieces)),
                dma((2 * layers,)),
                dma((n_orb - 1, width // unit)),
                dma((n_orb,)),
                dma((n_orb,)),
            ],
            compiler_params=pltpu.CompilerParams(
                collective_id=0, has_side_effects=True, vmem_limit_bytes=60 * 1024 * 1024
            ),
            cost_estimate=pl.CostEstimate(
                flops=2 * rows * depth * n_grid * mu,
                bytes_accessed=rows * depth * 2 + rows * width * 4,
                transcendentals=0,
            ),
        )(points.reshape(1, mu), orbitals)
        fitted, gram, density = pl.pallas_call(
            copies,
            out_shape=tuple(jax.ShapeDtypeStruct(m.shape, m.dtype) for m in made),
            in_specs=[pl.BlockSpec(memory_space=pl.ANY)] * 3,
            out_specs=(pl.BlockSpec(memory_space=pl.ANY),) * 3,
            scratch_shapes=[pltpu.VMEM(m.shape, m.dtype) for m in made] + [dma((6,))],
            compiler_params=pltpu.CompilerParams(vmem_limit_bytes=60 * 1024 * 1024),
        )(*made)
        return fitted, gram, density.reshape(mu)

    return jax.shard_map(
        on_device,
        mesh=mesh,
        in_specs=(P("grid", "orb"), P("grid")),
        out_specs=(P("grid", "orb"), P("grid", "orb"), P("grid")),
        check_vma=False,
    )
```
